32 devices in a mesh: grp: 2 (over x), slot: 4 (over y, core), site: 4 (over z).
Axes of the slice: x: 2, y: 2, z: 4, core: 2. Of those that a mesh axis runs over, the one named last changes fastest.
Arguments:
- field: bfloat16 [8, 2048, 4096], P('grp', 'slot', 'site'), parts along dimension 0, may hold values from -6 to 6
- time_row: bfloat16 [2048], replicated, may hold values from -0.125 to 0.125
- sp_weight: bfloat16 [4096, 2048], P('site'), may hold values from -0.1875 to 0.1875
- offsets: int32 [4096], P('site'), may hold values from 0 to 1024
- noise: float32 [4096], P('site'), may hold values from 0.1 to 1
Outputs:
- image: bfloat16 [8, 2048, 4096], P('grp', 'slot', 'site'), parts along dimension 0
The draws below stay inside these ranges and needn't reach their ends.
There are 2 independent parts, one for each index of `grp`. The reference program is written for one: setup_inputs(seed, part) draws one part's arguments, and reference() takes and returns one part's arrays. A program takes and returns all parts, laid end to end along the dimension named above; an argument that names none is the same for every part. Nothing has to cross between parts.
All inputs are finite; a program needn't handle non-finite values.
Results may differ from the reference program's by a relative error of at most 0.0048.
Values may be sent and summed in bfloat16 or wider, within the bound.
No kernel may reach another device: no remote copies, remote signals or barrier semaphores. Data moves between devices by JAX's collectives and lax.ppermute only.
A program may use at most 128 MiB of HBM per device.

```python
import math
import jax
import jax.numpy as jnp
from jax import lax

SLOTS = 2048
SITE_DEV = 1024
PROBES = 4
SITES = 4096
HALF = 512
PATCH = 2048
N_SITE = 4


def plant(array, key, low, largest):
    place = [jax.random.randint(jax.random.fold_in(key, axis), (), 0, length) for axis, length in enumerate(array.shape)]
    longest = array.shape.index(max(array.shape))
    neighbour = place[:longest] + [(place[longest] + 1) % array.shape[longest]] + place[longest + 1:]
    return array.at[tuple(place)].set(low).at[tuple(neighbour)].set(largest)


def levels(stream_key, dims, pieces, smallest, high):
    loudness = 1.0
    for dim, parts in pieces:
        draws = jax.random.uniform(jax.random.fold_in(jax.random.fold_in(stream_key, 6), dim), (parts,), jnp.float32, smallest / len(pieces), high / len(pieces))
        loudness = loudness * jnp.repeat(jnp.exp(draws), dims[dim] // parts).reshape((-1,) + (1,) * (len(dims) - 1 - dim))
    return loudness


def normal_values(stream_key, dims, width, reach, shards=(), held_as=jnp.bfloat16):
    factor_of = levels(stream_key, dims, shards, -0.22, 0.18) if shards else 1.0
    result = jax.random.normal(stream_key, dims, jnp.float32) * width * factor_of
    return jnp.minimum(jnp.maximum(result, -reach), reach).astype(held_as)


def setup_inputs(seed: int = 0, part: int = 0) -> dict:
    key_list = jax.random.split(jax.random.key(seed), 6)
    own_keys = jax.random.split(jax.random.fold_in(key_list[5], part), 6)
    return {
        "field": normal_values(own_keys[0], (PROBES, SLOTS, SITES), 1.0, 6.0, ((1, 4), (2, 4))),
        "time_row": normal_values(key_list[1], (SLOTS,), SLOTS ** -0.5, 0.125),
        "sp_weight": normal_values(key_list[2], (SITES, PATCH), SITE_DEV ** -0.5, 0.1875, ((0, 4),)),
        "offsets": plant(jax.random.randint(key_list[3], (SITES,), 0, SITE_DEV + 1), jax.random.fold_in(key_list[3], 1), 0, SITE_DEV).astype(jnp.int32),
        "noise": jnp.clip(jnp.exp(math.log(1.0) - 2.3025851 * jax.random.uniform(key_list[4], (SITES,), jnp.float32) ** levels(key_list[4], (SITES,), ((0, 4),), -0.2, 0.2)), 0.1, 1.0),
    }


def circulant(time_row):
    index = jnp.arange(SLOTS, dtype=jnp.int32)
    lag_table = (index[:, None] - index[None, :]) % SLOTS
    return jnp.take(time_row, lag_table, axis=0)


def reference(field, time_row, sp_weight, offsets, noise):
    kernel = circulant(time_row).astype(jnp.float32)

    def one_probe(plane):
        return jnp.dot(kernel, plane.astype(jnp.float32), precision=lax.Precision.HIGHEST).astype(jnp.bfloat16)

    mixed = lax.map(one_probe, field)
    padded = jnp.pad(mixed, ((0, 0), (0, 0), (HALF, HALF)))
    col_index = jnp.arange(PATCH, dtype=jnp.int32)

    def one_tile(tile):
        start = (tile * SITE_DEV).astype(jnp.int32)
        window = lax.dynamic_slice_in_dim(padded, start, PATCH, 2).astype(jnp.float32)
        weights = lax.dynamic_slice_in_dim(sp_weight, start, SITE_DEV, 0)
        starts = lax.dynamic_slice_in_dim(offsets, start, SITE_DEV, 0)
        band_mask = (col_index[None, :] >= starts[:, None]) & (col_index[None, :] < starts[:, None] + SITE_DEV)
        band = jnp.where(band_mask, weights, jnp.zeros_like(weights)).astype(jnp.float32)
        return jnp.einsum('ptj,sj->pts', window, band, precision=lax.Precision.HIGHEST)

    tiles = lax.map(one_tile, jnp.arange(N_SITE, dtype=jnp.int32))
    spatial = jnp.moveaxis(tiles, 0, 2).reshape(PROBES, SLOTS, SITES)
    image = spatial + noise[None, None, :] * field.astype(jnp.float32)
    return image.astype(jnp.bfloat16)
```

```python
import functools

import jax
import jax.numpy as jnp
from jax import lax
from jax.experimental import pallas as pl
from jax.experimental.pallas import tpu as pltpu
from jax.sharding import PartitionSpec as P

F32 = jnp.float32
BF16 = jnp.bfloat16
VMEM_BYTES = 24 * 1024 * 1024


def dot(a, b):
    return lax.dot_general(a, b, (((1,), (0,)), ((), ())), preferred_element_type=F32)


def dot_t(a, b):
    return lax.dot_general(a, b, (((1,), (1,)), ((), ())), preferred_element_type=F32)


def params():
    return pltpu.CompilerParams(vmem_limit_bytes=VMEM_BYTES)


BRIEF = pl.CostEstimate(flops=0, bytes_accessed=0, transcendentals=0)


def table_kernel(order, rows, core_ref, row_ref, out_ref):
    first = core_ref[0] == 0
    length = row_ref.shape[1]
    lags = pltpu.roll(jnp.broadcast_to(row_ref[...], (16, length)), 0, 1, stride=1, stride_axis=0)

    def group(g, carry):
        base = g * 16
        whole = pltpu.roll(lags, base, 1)
        for m, (a, b) in enumerate(zip(*order)):
            left = whole[:, a * rows : (a + 1) * rows]
            right = whole[:, b * rows : (b + 1) * rows]
            picked = left if a == b else jnp.where(first, left, right)
            out_ref[pl.ds(pl.multiple_of(base, 16), 16), m * rows : (m + 1) * rows] = picked.astype(BF16)
        return carry

    lax.fori_loop(0, rows // 16, group, 0)


def time_table(time_row, core, order, rows):
    reversed_row = jnp.concatenate([time_row[:1], time_row[1:][::-1]]).astype(F32)[None, :]
    length = time_row.shape[0]
    return pl.pallas_call(
        functools.partial(table_kernel, order, rows),
        out_shape=jax.ShapeDtypeStruct((rows, length), BF16),
        in_specs=[
            pl.BlockSpec(memory_space=pltpu.SMEM),
            pl.BlockSpec(memory_space=pltpu.VMEM),
        ],
        out_specs=pl.BlockSpec(memory_space=pltpu.VMEM),
        compiler_params=params(),
        cost_estimate=BRIEF,
        name="time_table",
    )(core, reversed_row)


ANY = pl.BlockSpec(memory_space=pl.ANY)


def space_kernel(half, noisy, *refs):
    low, mid, high, band = refs[:4]
    out = refs[-1]
    width = mid.shape[2]
    total = dot_t(mid[0], band[:, half : half + width])
    total += dot_t(low[0], band[:, :half])
    total += dot_t(high[0], band[:, half + width :])
    if noisy:
        noise, own = refs[4:6]
        total += noise[...] * own[0].astype(F32)
        out[0] = total.astype(BF16)
    else:
        out[...] = total.astype(BF16)


def space(low, mid, high, band, base, start, size, image=None):
    rows, width = mid.shape[1:]
    half = low.shape[2]
    step = min(256, size)
    skip, per = start // step, width // step

    def probe(j):
        return lax.div(j + skip, per)

    def site(j):
        return lax.rem(j + skip, per)

    args = [low, mid, high, band]
    specs = [
        pl.BlockSpec((1, rows, half), lambda j: (probe(j), 0, 0)),
        pl.BlockSpec((1, rows, width), lambda j: (probe(j) + base, 0, 0)),
        pl.BlockSpec((1, rows, half), lambda j: (probe(j), 0, 0)),
        pl.BlockSpec((step, band.shape[1]), lambda j: (site(j), 0)),
    ]
    aliases = {}
    if image is not None:
        noise, field, first, old = image
        args += [noise, field]
        out_spec = pl.BlockSpec((1, rows, step), lambda j: (probe(j) + first, 0, site(j)))
        specs += [pl.BlockSpec((1, step), lambda j: (0, site(j))), out_spec]
        if old is not None:
            args.append(old)
            specs.append(ANY)
            aliases = {len(args) - 1: 0}
        out_shape = jax.ShapeDtypeStruct(field.shape, BF16)
    else:
        out_shape = jax.ShapeDtypeStruct((rows, size), BF16)
        out_spec = pl.BlockSpec((rows, step), lambda j: (0, j))
    return pl.pallas_call(
        functools.partial(space_kernel, half, image is not None),
        grid=(size // step,),
        out_shape=out_shape,
        in_specs=specs,
        out_specs=out_spec,
        input_output_aliases=aliases,
        compiler_params=params(),
        cost_estimate=BRIEF,
        name="space",
    )(*args)


def mix_kernel(count, noisy, *refs):
    table = refs[0]
    blocks = refs[1 : 1 + count]
    out = refs[-1]
    rows = blocks[0].shape[0]
    total = dot(table[:, :rows], blocks[0][...])
    for m in range(1, count):
        total += dot(table[:, m * rows : (m + 1) * rows], blocks[m][...])
    if noisy:
        noise, own = refs[1 + count : 3 + count]
        total += noise[...] * own[0].astype(F32)
    out[0] = total.astype(BF16)


def mix(table, blocks, image=None):
    rows, width = blocks[0].shape
    step = min(512, width)
    args = [table] + list(blocks)
    specs = [pl.BlockSpec(table.shape, lambda j: (0, 0))]
    specs += [pl.BlockSpec((rows, step), lambda j: (0, j))] * len(blocks)
    aliases = {}
    if image is not None:
        noise, field, base, start, old = image
        skip, per = start // step, field.shape[2] // step

        def probe(j):
            return lax.div(j + skip, per) + base

        def site(j):
            return lax.rem(j + skip, per)

        args += [noise, field, old]
        out_spec = pl.BlockSpec((1, rows, step), lambda j: (probe(j), 0, site(j)))
        specs += [pl.BlockSpec((1, step), lambda j: (0, site(j))), out_spec, ANY]
        aliases = {len(args) - 1: 0}
        out_shape = jax.ShapeDtypeStruct(field.shape, BF16)
    else:
        out_shape = jax.ShapeDtypeStruct((1, rows, width), BF16)
        out_spec = pl.BlockSpec((1, rows, step), lambda j: (0, 0, j))
    return pl.pallas_call(
        functools.partial(mix_kernel, len(blocks), image is not None),
        grid=(width // step,),
        out_shape=out_shape,
        in_specs=specs,
        out_specs=out_spec,
        input_output_aliases=aliases,
        compiler_params=params(),
        cost_estimate=BRIEF,
        name="mix",
    )(*args)


def after(value, *others):
    return lax.optimization_barrier((value,) + others)[0]


def on_device(field, time_row, sp_weight, offsets, noise):
    probes, rows, width = field.shape
    half = width // 2
    count = lax.axis_size("slot")
    sites = lax.axis_size("site")
    core = (lax.axis_index("slot") % 2).astype(jnp.int32).reshape(1)
    noise = noise[None, :]

    swap = [(i, i ^ 1) for i in range(count)]
    shifts = range(2, count, 2)
    up = [(i, i + 1) for i in range(sites - 1)]
    down = [(i + 1, i) for i in range(sites - 1)]

    def to_core(block):
        return lax.ppermute(block, "slot", swap)

    def to_chips(block):
        return [lax.ppermute(block, "slot", [(i, (i + s) % count) for i in range(count)]) for s in shifts]

    def halo(block):
        return (
            lax.ppermute(block[:, :, width - half :], "site", up),
            lax.ppermute(block[:, :, :half], "site", down),
        )

    order = ([0, 1], [0, count - 1])
    for s in shifts:
        order[0].extend([(-s) % count, (1 - s) % count])
        order[1].extend([(-s) % count, (-1 - s) % count])

    def gathered(own, far, *others):
        blocks = [own, to_core(own)]
        for got in far:
            got = after(got, *others)
            blocks += [got, to_core(got)]
        return blocks

    firsts = probes // 2
    own, far = [], []
    rest = field
    for p in range(firsts):
        own.append(rest[p])
        far.append(to_chips(own[p]))
        rest = after(field, own[p])
        if p == 0:
            low, high = halo(rest[firsts:])

    table = time_table(time_row, core, order, rows)
    col = jnp.arange(sp_weight.shape[1], dtype=jnp.int32)
    mask = (col[None, :] >= offsets[:, None]) & (col[None, :] < offsets[:, None] + width)
    band = jnp.where(mask, sp_weight, jnp.zeros_like(sp_weight))

    mixed = [mix(table, gathered(own[0], far[0]))]
    columns = (probes - firsts) * width
    chunks = [(0, columns - half), (columns - half, half)]
    sent = []
    weights = band
    for start, size in chunks:
        block = space(low, field, high, weights, firsts, start, size)
        sent.append((block, to_chips(block)))
        weights = after(band, block)
    for p in range(1, firsts):
        mixed.append(mix(table, gathered(own[p], far[p], mixed[-1], block)))

    image = None
    for p in range(firsts):
        got_low, got_high = halo(mixed[p])
        image = space(got_low, mixed[p], got_high, band, 0, 0, width, image=(noise, field, p, image))
    for (start, _), (block, got) in zip(chunks, sent):
        image = mix(table, gathered(block, got, image), image=(noise, field, firsts, start, image))
    return image


def solution(mesh):
    in_specs = (P("grp", "slot", "site"), P(), P("site", None), P("site"), P("site"))
    out_specs = P("grp", "slot", "site")
    return jax.shard_map(
        on_device, mesh=mesh, in_specs=in_specs, out_specs=out_specs, check_vma=False
    )
```

```python
import functools

import jax
import jax.numpy as jnp
from jax import lax
from jax.experimental import pallas as pl
from jax.experimental.pallas import tpu as pltpu
from jax.sharding import PartitionSpec as P

F32 = jnp.float32
BF16 = jnp.bfloat16
VMEM_BYTES = 24 * 1024 * 1024


def dot(a, b):
    return lax.dot_general(a, b, (((1,), (0,)), ((), ())), preferred_element_type=F32)


def dot_t(a, b):
    return lax.dot_general(a, b, (((1,), (1,)), ((), ())), preferred_element_type=F32)


def params():
    return pltpu.CompilerParams(vmem_limit_bytes=VMEM_BYTES)


BRIEF = pl.CostEstimate(flops=0, bytes_accessed=0, transcendentals=0)


def table_kernel(order, rows, core_ref, row_ref, out_ref):
    first = core_ref[0] == 0
    length = row_ref.shape[1]
    lags = pltpu.roll(jnp.broadcast_to(row_ref[...], (16, length)), 0, 1, stride=1, stride_axis=0)

    def group(g, carry):
        base = g * 16
        whole = pltpu.roll(lags, base, 1)
        for m, (a, b) in enumerate(zip(*order)):
            left = whole[:, a * rows : (a + 1) * rows]
            right = whole[:, b * rows : (b + 1) * rows]
            picked = left if a == b else jnp.where(first, left, right)
            out_ref[pl.ds(pl.multiple_of(base, 16), 16), m * rows : (m + 1) * rows] = picked.astype(BF16)
        return carry

    lax.fori_loop(0, rows // 16, group, 0)


def time_table(time_row, core, order, rows):
    reversed_row = jnp.concatenate([time_row[:1], time_row[1:][::-1]]).astype(F32)[None, :]
    length = time_row.shape[0]
    return pl.pallas_call(
        functools.partial(table_kernel, order, rows),
        out_shape=jax.ShapeDtypeStruct((rows, length), BF16),
        in_specs=[
            pl.BlockSpec(memory_space=pltpu.SMEM),
            pl.BlockSpec(memory_space=pltpu.VMEM),
        ],
        out_specs=pl.BlockSpec(memory_space=pltpu.VMEM),
        compiler_params=params(),
        cost_estimate=BRIEF,
        name="time_table",
    )(core, reversed_row)


ANY = pl.BlockSpec(memory_space=pl.ANY)


def space_kernel(half, noisy, *refs):
    low, mid, high, band = refs[:4]
    out = refs[-1]
    width = mid.shape[2]
    total = dot_t(mid[0], band[:, half : half + width])
    total += dot_t(low[0], band[:, :half])
    total += dot_t(high[0], band[:, half + width :])
    if noisy:
        noise, own = refs[4:6]
        total += noise[...] * own[0].astype(F32)
        out[0] = total.astype(BF16)
    else:
        out[...] = total.astype(BF16)


def space(low, mid, high, band, base, start, size, image=None):
    rows, width = mid.shape[1:]
    half = low.shape[2]
    step = min(256, size)
    skip, per = start // step, width // step

    def probe(j):
        return lax.div(j + skip, per)

    def site(j):
        return lax.rem(j + skip, per)

    args = [low, mid, high, band]
    specs = [
        pl.BlockSpec((1, rows, half), lambda j: (probe(j), 0, 0)),
        pl.BlockSpec((1, rows, width), lambda j: (probe(j) + base, 0, 0)),
        pl.BlockSpec((1, rows, half), lambda j: (probe(j), 0, 0)),
        pl.BlockSpec((step, band.shape[1]), lambda j: (site(j), 0)),
    ]
    aliases = {}
    if image is not None:
        noise, field, first, old = image
        args += [noise, field]
        out_spec = pl.BlockSpec((1, rows, step), lambda j: (probe(j) + first, 0, site(j)))
        specs += [pl.BlockSpec((1, step), lambda j: (0, site(j))), out_spec]
        if old is not None:
            args.append(old)
            specs.append(ANY)
            aliases = {len(args) - 1: 0}
        out_shape = jax.ShapeDtypeStruct(field.shape, BF16)
    else:
        out_shape = jax.ShapeDtypeStruct((rows, size), BF16)
        out_spec = pl.BlockSpec((rows, step), lambda j: (0, j))
    return pl.pallas_call(
        functools.partial(space_kernel, half, image is not None),
        grid=(size // step,),
        out_shape=out_shape,
        in_specs=specs,
        out_specs=out_spec,
        input_output_aliases=aliases,
        compiler_params=params(),
        cost_estimate=BRIEF,
        name="space",
    )(*args)


def mix_kernel(pieces, noisy, *refs):
    table = refs[0]
    out = refs[-1]
    taken = 1
    total = None
    for m, count in enumerate(pieces):
        block = jnp.concatenate([ref[...] for ref in refs[taken : taken + count]], axis=0)
        taken += count
        rows = block.shape[0]
        term = dot(table[:, m * rows : (m + 1) * rows], block)
        total = term if total is None else total + term
    if noisy:
        noise, own = refs[taken : taken + 2]
        total += noise[...] * own[0].astype(F32)
    out[0] = total.astype(BF16)


def mix(table, blocks, image=None):
    rows, width = blocks[0][0].shape
    step = min(512, width)
    flat = [piece for block in blocks for piece in block]
    args = [table] + flat
    specs = [pl.BlockSpec(table.shape, lambda j: (0, 0))]
    specs += [pl.BlockSpec((piece.shape[0], step), lambda j: (0, j)) for piece in flat]
    aliases = {}
    if image is not None:
        noise, field, base, start, old = image
        skip, per = start // step, field.shape[2] // step

        def probe(j):
            return lax.div(j + skip, per) + base

        def site(j):
            return lax.rem(j + skip, per)

        args += [noise, field, old]
        out_spec = pl.BlockSpec((1, rows, step), lambda j: (probe(j), 0, site(j)))
        specs += [pl.BlockSpec((1, step), lambda j: (0, site(j))), out_spec, ANY]
        aliases = {len(args) - 1: 0}
        out_shape = jax.ShapeDtypeStruct(field.shape, BF16)
    else:
        out_shape = jax.ShapeDtypeStruct((1, rows, width), BF16)
        out_spec = pl.BlockSpec((1, rows, step), lambda j: (0, 0, j))
    return pl.pallas_call(
        functools.partial(mix_kernel, [len(block) for block in blocks], image is not None),
        grid=(width // step,),
        out_shape=out_shape,
        in_specs=specs,
        out_specs=out_spec,
        input_output_aliases=aliases,
        compiler_params=params(),
        cost_estimate=BRIEF,
        name="mix",
    )(*args)


def after(value, *others):
    return lax.optimization_barrier((value,) + others)[0]


def on_device(field, time_row, sp_weight, offsets, noise):
    probes, rows, width = field.shape
    half = width // 2
    count = lax.axis_size("slot")
    sites = lax.axis_size("site")
    core = (lax.axis_index("slot") % 2).astype(jnp.int32).reshape(1)
    noise = noise[None, :]

    swap = [(i, i ^ 1) for i in range(count)]
    shifts = range(2, count, 2)
    up = [(i, i + 1) for i in range(sites - 1)]
    down = [(i + 1, i) for i in range(sites - 1)]

    def to_core(block):
        return lax.ppermute(block, "slot", swap)

    def to_chips(block):
        return [lax.ppermute(block, "slot", [(i, (i + s) % count) for i in range(count)]) for s in shifts]

    def halo(block):
        return (
            lax.ppermute(block[:, :, width - half :], "site", up),
            lax.ppermute(block[:, :, :half], "site", down),
        )

    order = ([0, 1], [0, count - 1])
    for s in shifts:
        order[0].extend([(-s) % count, (1 - s) % count])
        order[1].extend([(-s) % count, (-1 - s) % count])

    def gathered(own, far, pieces, *others):
        blocks = [[own], [to_core(own)]]
        for got in far:
            got = after(got, *others)
            blocks += [[got], [to_core(part) for part in jnp.split(got, pieces, axis=0)]]
        return blocks

    firsts = probes // 2
    own, far = [], []
    rest = field
    for p in range(firsts):
        own.append(rest[p])
        far.append(to_chips(own[p]))
        rest = after(field, own[p])
        if p == 0:
            low, high = halo(rest[firsts:])

    table = time_table(time_row, core, order, rows)
    col = jnp.arange(sp_weight.shape[1], dtype=jnp.int32)
    mask = (col[None, :] >= offsets[:, None]) & (col[None, :] < offsets[:, None] + width)
    band = jnp.where(mask, sp_weight, jnp.zeros_like(sp_weight))

    columns = (probes - firsts) * width
    mixed = [mix(table, gathered(own[0], far[0], 2, table, band))]
    long = space(low, field, high, after(band, mixed[0]), firsts, 0, columns - half)
    sent = [(0, long, to_chips(long), 4)]
    for p in range(1, firsts):
        mixed.append(mix(table, gathered(own[p], far[p], 2, mixed[-1], long)))

    image = None
    for p in range(firsts):
        got_low, got_high = halo(mixed[p])
        image = space(got_low, mixed[p], got_high, band, 0, 0, width, image=(noise, field, p, image))
        if p == 0:
            short = space(low, field, high, after(band, image), firsts, columns - half, half)
            sent.append((columns - half, short, to_chips(short), 1))
    for start, block, got, pieces in sent:
        image = mix(table, gathered(block, got, pieces, image), image=(noise, field, firsts, start, image))
    return image


def solution(mesh):
    in_specs = (P("grp", "slot", "site"), P(), P("site", None), P("site"), P("site"))
    out_specs = P("grp", "slot", "site")
    return jax.shard_map(
        on_device, mesh=mesh, in_specs=in_specs, out_specs=out_specs, check_vma=False
    )
```

```python
import functools

import jax
import jax.numpy as jnp
from jax import lax
from jax.experimental import pallas as pl
from jax.experimental.pallas import tpu as pltpu
from jax.sharding import PartitionSpec as P

F32 = jnp.float32
BF16 = jnp.bfloat16
VMEM_BYTES = 24 * 1024 * 1024


def dot(a, b):
    return lax.dot_general(a, b, (((1,), (0,)), ((), ())), preferred_element_type=F32)


def dot_t(a, b):
    return lax.dot_general(a, b, (((1,), (1,)), ((), ())), preferred_element_type=F32)


def params():
    return pltpu.CompilerParams(vmem_limit_bytes=VMEM_BYTES)


BRIEF = pl.CostEstimate(flops=0, bytes_accessed=0, transcendentals=0)


def table_kernel(order, rows, core_ref, row_ref, out_ref):
    first = core_ref[0] == 0
    length = row_ref.shape[1]
    lags = pltpu.roll(jnp.broadcast_to(row_ref[...], (16, length)), 0, 1, stride=1, stride_axis=0)

    def group(g, carry):
        base = g * 16
        whole = pltpu.roll(lags, base, 1)
        for m, (a, b) in enumerate(zip(*order)):
            left = whole[:, a * rows : (a + 1) * rows]
            right = whole[:, b * rows : (b + 1) * rows]
            picked = left if a == b else jnp.where(first, left, right)
            out_ref[pl.ds(pl.multiple_of(base, 16), 16), m * rows : (m + 1) * rows] = picked.astype(BF16)
        return carry

    lax.fori_loop(0, rows // 16, group, 0)


def time_table(time_row, core, order, rows):
    reversed_row = jnp.concatenate([time_row[:1], time_row[1:][::-1]]).astype(F32)[None, :]
    length = time_row.shape[0]
    return pl.pallas_call(
        functools.partial(table_kernel, order, rows),
        out_shape=jax.ShapeDtypeStruct((rows, length), BF16),
        in_specs=[
            pl.BlockSpec(memory_space=pltpu.SMEM),
            pl.BlockSpec(memory_space=pltpu.VMEM),
        ],
        out_specs=pl.BlockSpec(memory_space=pltpu.VMEM),
        compiler_params=params(),
        cost_estimate=BRIEF,
        name="time_table",
    )(core, reversed_row)


ANY = pl.BlockSpec(memory_space=pl.ANY)


def space_kernel(half, noisy, *refs):
    low, mid, high, band = refs[:4]
    out = refs[-1]
    width = mid.shape[2]
    total = dot_t(mid[0], band[:, half : half + width])
    total += dot_t(low[0], band[:, :half])
    total += dot_t(high[0], band[:, half + width :])
    if noisy:
        noise, own = refs[4:6]
        total += noise[...] * own[0].astype(F32)
        out[0] = total.astype(BF16)
    else:
        out[...] = total.astype(BF16)


def space(low, mid, high, band, base, start, size, image=None):
    rows, width = mid.shape[1:]
    half = low.shape[2]
    step = min(256, size)
    skip, per = start // step, width // step

    def probe(j):
        return lax.div(j + skip, per)

    def site(j):
        return lax.rem(j + skip, per)

    args = [low, mid, high, band]
    specs = [
        pl.BlockSpec((1, rows, half), lambda j: (probe(j), 0, 0)),
        pl.BlockSpec((1, rows, width), lambda j: (probe(j) + base, 0, 0)),
        pl.BlockSpec((1, rows, half), lambda j: (probe(j), 0, 0)),
        pl.BlockSpec((step, band.shape[1]), lambda j: (site(j), 0)),
    ]
    aliases = {}
    if image is not None:
        noise, field, first, old = image
        args += [noise, field]
        out_spec = pl.BlockSpec((1, rows, step), lambda j: (probe(j) + first, 0, site(j)))
        specs += [pl.BlockSpec((1, step), lambda j: (0, site(j))), out_spec]
        if old is not None:
            args.append(old)
            specs.append(ANY)
            aliases = {len(args) - 1: 0}
        out_shape = jax.ShapeDtypeStruct(field.shape, BF16)
    else:
        out_shape = jax.ShapeDtypeStruct((rows, size), BF16)
        out_spec = pl.BlockSpec((rows, step), lambda j: (0, j))
    return pl.pallas_call(
        functools.partial(space_kernel, half, image is not None),
        grid=(size // step,),
        out_shape=out_shape,
        in_specs=specs,
        out_specs=out_spec,
        input_output_aliases=aliases,
        compiler_params=params(),
        cost_estimate=BRIEF,
        name="space",
    )(*args)


def mix_kernel(pieces, noisy, *refs):
    table = refs[0]
    out = refs[-1]
    taken = 1
    total = None
    for m, count in enumerate(pieces):
        block = jnp.concatenate([ref[...] for ref in refs[taken : taken + count]], axis=0)
        taken += count
        rows = block.shape[0]
        term = dot(table[:, m * rows : (m + 1) * rows], block)
        total = term if total is None else total + term
    if noisy:
        noise, own = refs[taken : taken + 2]
        total += noise[...] * own[0].astype(F32)
    out[0] = total.astype(BF16)


def mix(table, blocks, image=None):
    rows, width = blocks[0][0].shape
    step = min(512, width)
    flat = [piece for block in blocks for piece in block]
    args = [table] + flat
    specs = [pl.BlockSpec(table.shape, lambda j: (0, 0))]
    specs += [pl.BlockSpec((piece.shape[0], step), lambda j: (0, j)) for piece in flat]
    aliases = {}
    if image is not None:
        noise, field, base, start, old = image
        skip, per = start // step, field.shape[2] // step

        def probe(j):
            return lax.div(j + skip, per) + base

        def site(j):
            return lax.rem(j + skip, per)

        args += [noise, field, old]
        out_spec = pl.BlockSpec((1, rows, step), lambda j: (probe(j), 0, site(j)))
        specs += [pl.BlockSpec((1, step), lambda j: (0, site(j))), out_spec, ANY]
        aliases = {len(args) - 1: 0}
        out_shape = jax.ShapeDtypeStruct(field.shape, BF16)
    else:
        out_shape = jax.ShapeDtypeStruct((1, rows, width), BF16)
        out_spec = pl.BlockSpec((1, rows, step), lambda j: (0, 0, j))
    return pl.pallas_call(
        functools.partial(mix_kernel, [len(block) for block in blocks], image is not None),
        grid=(width // step,),
        out_shape=out_shape,
        in_specs=specs,
        out_specs=out_spec,
        input_output_aliases=aliases,
        compiler_params=params(),
        cost_estimate=BRIEF,
        name="mix",
    )(*args)


def after(value, *others):
    return lax.optimization_barrier((value,) + others)[0]


def on_device(field, time_row, sp_weight, offsets, noise):
    probes, rows, width = field.shape
    half = width // 2
    count = lax.axis_size("slot")
    sites = lax.axis_size("site")
    core = (lax.axis_index("slot") % 2).astype(jnp.int32).reshape(1)
    noise = noise[None, :]

    swap = [(i, i ^ 1) for i in range(count)]
    shifts = range(2, count, 2)
    up = [(i, i + 1) for i in range(sites - 1)]
    down = [(i + 1, i) for i in range(sites - 1)]

    def to_core(block, pieces=1):
        return [lax.ppermute(part, "slot", swap) for part in jnp.split(block, pieces, axis=0)]

    def to_chips(block):
        return [lax.ppermute(block, "slot", [(i, (i + s) % count) for i in range(count)]) for s in shifts]

    def halo(block):
        return (
            lax.ppermute(block[:, :, width - half :], "site", up),
            lax.ppermute(block[:, :, :half], "site", down),
        )

    order = ([0, 1], [0, count - 1])
    for s in shifts:
        order[0].extend([(-s) % count, (1 - s) % count])
        order[1].extend([(-s) % count, (-1 - s) % count])

    def gathered(own, near, far, pieces, *others):
        blocks = [[own], near]
        for got in far:
            got = after(got, *others)
            blocks += [[got], to_core(got, pieces)]
        return blocks

    firsts = probes // 2
    own, far = [], []
    rest = field
    for p in range(firsts):
        own.append(rest[p])
        far.append(to_chips(own[p]))
        rest = after(field, own[p])
        if p == 0:
            low, high = halo(rest[firsts:])

    table = time_table(time_row, core, order, rows)
    col = jnp.arange(sp_weight.shape[1], dtype=jnp.int32)
    mask = (col[None, :] >= offsets[:, None]) & (col[None, :] < offsets[:, None] + width)
    band = jnp.where(mask, sp_weight, jnp.zeros_like(sp_weight))

    near = [to_core(block) for block in own]
    columns = (probes - firsts) * width
    mixed = [mix(table, gathered(own[0], near[0], far[0], 2, table, band))]
    long = space(low, field, high, after(band, mixed[0]), firsts, 0, columns - half)
    far_long = to_chips(long)
    for p in range(1, firsts):
        mixed.append(mix(table, gathered(own[p], near[p], far[p], 2, mixed[-1], long)))

    image = None
    for p in range(firsts):
        got_low, got_high = halo(mixed[p])
        image = space(got_low, mixed[p], got_high, band, 0, 0, width, image=(noise, field, p, image))
        if p == 0:
            near_long = to_core(after(long, image), 4)
            short = space(low, field, high, after(band, image), firsts, columns - half, half)
            near_short, far_short = to_core(short), to_chips(short)
    for start, block, beside, got, pieces in (
        (0, long, near_long, far_long, 4),
        (columns - half, short, near_short, far_short, 1),
    ):
        blocks = gathered(block, beside, got, pieces, image)
        image = mix(table, blocks, image=(noise, field, firsts, start, image))
    return image


def solution(mesh):
    in_specs = (P("grp", "slot", "site"), P(), P("site", None), P("site"), P("site"))
    out_specs = P("grp", "slot", "site")
    return jax.shard_map(
        on_device, mesh=mesh, in_specs=in_specs, out_specs=out_specs, check_vma=False
    )
```

```python
import functools

import jax
import jax.numpy as jnp
from jax import lax
from jax.experimental import pallas as pl
from jax.experimental.pallas import tpu as pltpu
from jax.sharding import PartitionSpec as P

F32 = jnp.float32
BF16 = jnp.bfloat16
VMEM_BYTES = 24 * 1024 * 1024


def dot(a, b):
    return lax.dot_general(a, b, (((1,), (0,)), ((), ())), preferred_element_type=F32)


def dot_t(a, b):
    return lax.dot_general(a, b, (((1,), (1,)), ((), ())), preferred_element_type=F32)


def params():
    return pltpu.CompilerParams(vmem_limit_bytes=VMEM_BYTES)


BRIEF = pl.CostEstimate(flops=0, bytes_accessed=0, transcendentals=0)


def table_kernel(order, rows, core_ref, row_ref, out_ref):
    first = core_ref[0] == 0
    length = row_ref.shape[1]
    lags = pltpu.roll(jnp.broadcast_to(row_ref[...], (16, length)), 0, 1, stride=1, stride_axis=0)

    def group(g, carry):
        base = g * 16
        whole = pltpu.roll(lags, base, 1)
        for m, (a, b) in enumerate(zip(*order)):
            left = whole[:, a * rows : (a + 1) * rows]
            right = whole[:, b * rows : (b + 1) * rows]
            picked = left if a == b else jnp.where(first, left, right)
            out_ref[pl.ds(pl.multiple_of(base, 16), 16), m * rows : (m + 1) * rows] = picked.astype(BF16)
        return carry

    lax.fori_loop(0, rows // 16, group, 0)


def time_table(time_row, core, order, rows):
    reversed_row = jnp.concatenate([time_row[:1], time_row[1:][::-1]]).astype(F32)[None, :]
    length = time_row.shape[0]
    return pl.pallas_call(
        functools.partial(table_kernel, order, rows),
        out_shape=jax.ShapeDtypeStruct((rows, length), BF16),
        in_specs=[
            pl.BlockSpec(memory_space=pltpu.SMEM),
            pl.BlockSpec(memory_space=pltpu.VMEM),
        ],
        out_specs=pl.BlockSpec(memory_space=pltpu.VMEM),
        compiler_params=params(),
        cost_estimate=BRIEF,
        name="time_table",
    )(core, reversed_row)


ANY = pl.BlockSpec(memory_space=pl.ANY)


def by_columns(name, body, args, rows, start, size, step, width, probe, terms=None, image=None, dtype=BF16):
    vmem = pl.BlockSpec(memory_space=pltpu.VMEM)
    args = list(args) + list(terms or ())
    specs = [vmem] * len(args)
    used = len(args)
    aliases, scratch = {}, []
    if image is None:
        out_shape = jax.ShapeDtypeStruct((rows, size), dtype)
        out_spec = vmem
    else:
        if not isinstance(image, jax.ShapeDtypeStruct):
            aliases = {used: 0}
            args.append(image)
            specs.append(ANY)
        out_shape = jax.ShapeDtypeStruct(image.shape, image.dtype)
        out_spec = ANY
        scratch = [
            pltpu.VMEM((size // step, rows, step), image.dtype),
            pltpu.SemaphoreType.DMA((size // step,)),
        ]

    def kernel(*refs):
        inputs, out = refs[:used], refs[len(args)]
        copies = []
        for index in range(size // step):
            column = start + index * step
            place, site = probe + column // width, column % width
            total = body(inputs, index * step, column // width, site)
            if terms is not None:
                noise, field = inputs[used - 2 :]
                total += noise[:, site : site + step] * field[place, :, site : site + step].astype(F32)
            if image is None:
                out[:, index * step : (index + 1) * step] = total.astype(dtype)
            else:
                buffer, sems = refs[len(args) + 1 :]
                buffer[index] = total.astype(image.dtype)
                copy = pltpu.make_async_copy(
                    buffer.at[index], out.at[place, :, pl.ds(site, step)], sems.at[index]
                )
                copy.start()
                copies.append(copy)
        for copy in copies:
            copy.wait()

    return pl.pallas_call(
        kernel,
        out_shape=out_shape,
        in_specs=specs,
        out_specs=out_spec,
        scratch_shapes=scratch,
        input_output_aliases=aliases,
        compiler_params=params(),
        cost_estimate=BRIEF,
        name=name,
    )(*args)


def space(low, mid, high, band, base, start, size, width, **where):
    half, step = width // 2, min(256, size)

    def body(refs, offset, probe, site):
        low, mid, high, band = refs[:4]
        weights = band.at[site : site + step]
        total = dot_t(mid[base + probe], weights[:, half : half + width])
        total += dot_t(low[probe], weights[:, :half])
        total += dot_t(high[probe], weights[:, half + width :])
        return total

    where = dict(dict(probe=0), **where)
    return by_columns("space", body, [low, mid, high, band], mid.shape[1], start, size, step, width, **where)


def mix(table, blocks, width, start=0, begun=None, step=512, **where):
    rows = table.shape[0]
    flat = [piece for block in blocks.values() for piece in block]
    size = flat[0].shape[1]
    step = min(step, size)

    def body(refs, offset, probe, site):
        columns = slice(offset, offset + step)
        taken = 1
        total = None
        for m, block in blocks.items():
            parts = [ref[:, columns] for ref in refs[taken : taken + len(block)]]
            taken += len(block)
            term = dot(refs[0][:, m * rows : (m + 1) * rows], jnp.concatenate(parts, axis=0))
            total = term if total is None else total + term
        return total if begun is None else total + refs[taken][:, columns]

    args = [table] + flat + ([] if begun is None else [begun])
    where = dict(dict(probe=0), **where)
    return by_columns("mix", body, args, rows, start, size, step, width, **where)


def after(value, *others):
    return lax.optimization_barrier((value,) + others)[0]


def on_device(field, time_row, sp_weight, offsets, noise):
    probes, rows, width = field.shape
    half = width // 2
    count = lax.axis_size("slot")
    sites = lax.axis_size("site")
    core = (lax.axis_index("slot") % 2).astype(jnp.int32).reshape(1)
    noise = noise[None, :]

    swap = [(i, i ^ 1) for i in range(count)]
    shifts = range(2, count, 2)
    up = [(i, i + 1) for i in range(sites - 1)]
    down = [(i + 1, i) for i in range(sites - 1)]

    def to_core(block, pieces=1):
        return [lax.ppermute(part, "slot", swap) for part in jnp.split(block, pieces, axis=0)]

    def to_chips(block):
        return [lax.ppermute(block, "slot", [(i, (i + s) % count) for i in range(count)]) for s in shifts]

    def halo(block):
        return (
            lax.ppermute(block[:, :, width - half :], "site", up),
            lax.ppermute(block[:, :, :half], "site", down),
        )

    order = ([0, 1], [0, count - 1])
    for s in shifts:
        order[0].extend([(-s) % count, (1 - s) % count])
        order[1].extend([(-s) % count, (-1 - s) % count])

    def arrived(far, pieces, *others):
        blocks = {}
        for k, got in enumerate(far):
            got = after(got, *others)
            blocks[2 + 2 * k] = [got]
            blocks[3 + 2 * k] = to_core(got, pieces)
        return blocks

    def here(own, near):
        return {0: [own], 1: near}

    firsts = probes // 2
    own, far = [], []
    rest = field
    for p in range(firsts):
        own.append(rest[p])
        far.append(to_chips(own[p]))
        rest = after(field, own[p])
        if p == 0:
            low, high = halo(rest[firsts:])

    table = time_table(time_row, core, order, rows)
    col = jnp.arange(sp_weight.shape[1], dtype=jnp.int32)
    mask = (col[None, :] >= offsets[:, None]) & (col[None, :] < offsets[:, None] + width)
    band = jnp.where(mask, sp_weight, jnp.zeros_like(sp_weight))

    near = [to_core(block) for block in own]
    columns = (probes - firsts) * width
    cut = columns - half
    terms = (noise, field)
    image = jax.ShapeDtypeStruct(field.shape, field.dtype)

    blocks = here(own[0], near[0]) | arrived(far[0], 2, table, band)
    mixed = [mix(table, blocks, width)]
    long = space(low, field, high, after(band, mixed[0]), firsts, 0, cut, width)
    far_long = to_chips(long)
    for p in range(1, firsts):
        blocks = here(own[p], near[p]) | arrived(far[p], 2, mixed[-1], long)
        mixed.append(mix(table, blocks, width))

    for p in range(firsts):
        middle = mixed[p][None]
        got_low, got_high = halo(middle)
        image = space(got_low, middle, got_high, band, 0, 0, width, width, probe=p, terms=terms, image=image)
        if p == 0:
            near_long = to_core(after(long, image), 4)
            short = space(low, field, high, after(band, image), firsts, cut, half, width)
            near_short, far_short = to_core(short), to_chips(short)

    at = dict(start=cut, probe=firsts)
    begun = mix(table, here(short, after(near_short, image)), width, terms=terms, dtype=F32, **at)
    blocks = here(long, near_long) | arrived(far_long, 4, begun)
    image = mix(table, blocks, width, probe=firsts, terms=terms, image=image)
    blocks = arrived(far_short, 1, image)
    straight = {m: block for m, block in blocks.items() if m % 2 == 0}
    crossed = {m: block for m, block in blocks.items() if m % 2 == 1}
    begun = mix(table, straight, width, begun=begun, dtype=F32, **at)
    return mix(table, crossed, width, begun=begun, image=image, step=256, **at)


def solution(mesh):
    in_specs = (P("grp", "slot", "site"), P(), P("site", None), P("site"), P("site"))
    out_specs = P("grp", "slot", "site")
    return jax.shard_map(
        on_device, mesh=mesh, in_specs=in_specs, out_specs=out_specs, check_vma=False
    )
```

```python
import functools

import jax
import jax.numpy as jnp
from jax import lax
from jax.experimental import pallas as pl
from jax.experimental.pallas import tpu as pltpu
from jax.sharding import PartitionSpec as P

F32 = jnp.float32
BF16 = jnp.bfloat16
VMEM_BYTES = 24 * 1024 * 1024


def dot(a, b):
    return lax.dot_general(a, b, (((1,), (0,)), ((), ())), preferred_element_type=F32)


def dot_t(a, b):
    return lax.dot_general(a, b, (((1,), (1,)), ((), ())), preferred_element_type=F32)


def params():
    return pltpu.CompilerParams(vmem_limit_bytes=VMEM_BYTES)


BRIEF = pl.CostEstimate(flops=0, bytes_accessed=0, transcendentals=0)


def table_kernel(order, rows, core_ref, row_ref, out_ref):
    first = core_ref[0] == 0
    length = row_ref.shape[1]
    lags = pltpu.roll(jnp.broadcast_to(row_ref[...], (16, length)), 0, 1, stride=1, stride_axis=0)

    def group(g, carry):
        base = g * 16
        whole = pltpu.roll(lags, base, 1)
        for m, (a, b) in enumerate(zip(*order)):
            left = whole[:, a * rows : (a + 1) * rows]
            right = whole[:, b * rows : (b + 1) * rows]
            picked = left if a == b else jnp.where(first, left, right)
            out_ref[pl.ds(pl.multiple_of(base, 16), 16), m * rows : (m + 1) * rows] = picked.astype(BF16)
        return carry

    lax.fori_loop(0, rows // 16, group, 0)


def time_table(time_row, core, order, rows):
    reversed_row = jnp.concatenate([time_row[:1], time_row[1:][::-1]]).astype(F32)[None, :]
    length = time_row.shape[0]
    return pl.pallas_call(
        functools.partial(table_kernel, order, rows),
        out_shape=jax.ShapeDtypeStruct((rows, length), BF16),
        in_specs=[
            pl.BlockSpec(memory_space=pltpu.SMEM),
            pl.BlockSpec(memory_space=pltpu.VMEM),
        ],
        out_specs=pl.BlockSpec(memory_space=pltpu.VMEM),
        compiler_params=params(),
        cost_estimate=BRIEF,
        name="time_table",
    )(core, reversed_row)


ANY = pl.BlockSpec(memory_space=pl.ANY)


def by_columns(name, body, args, rows, start, size, step, width, probe=0, terms=None, image=None, dtype=BF16):
    vmem = pl.BlockSpec(memory_space=pltpu.VMEM)
    args = list(args) + list(terms or ())
    specs = [vmem] * len(args)
    used = len(args)
    blocks, column = [], start
    while column < start + size:
        length = min(step, width - column % width, start + size - column)
        blocks.append((slice(column - start, column - start + length), *divmod(column, width), length))
        column += length
    aliases, scratch = {}, []
    if image is None:
        out_shape = jax.ShapeDtypeStruct((rows, size), dtype)
        out_spec = vmem
    else:
        if not isinstance(image, jax.ShapeDtypeStruct):
            aliases = {used: 0}
            args.append(image)
            specs.append(ANY)
        out_shape = jax.ShapeDtypeStruct(image.shape, image.dtype)
        out_spec = ANY
        scratch = [pltpu.VMEM((rows, size), image.dtype), pltpu.SemaphoreType.DMA((len(blocks),))]

    def kernel(*refs):
        inputs, out = refs[:used], refs[len(args)]
        copies = []
        for index, (columns, offset, site, length) in enumerate(blocks):
            sites = slice(site, site + length)
            total = body(inputs, columns, offset, sites)
            if terms is not None:
                noise, field = inputs[used - 2 :]
                total += noise[:, sites] * field[probe + offset, :, sites].astype(F32)
            if image is None:
                out[:, columns] = total.astype(dtype)
            else:
                buffer, sems = refs[len(args) + 1 :]
                buffer[:, columns] = total.astype(image.dtype)
                copy = pltpu.make_async_copy(
                    buffer.at[:, columns], out.at[probe + offset, :, sites], sems.at[index]
                )
                copy.start()
                copies.append(copy)
        for copy in copies:
            copy.wait()

    return pl.pallas_call(
        kernel,
        out_shape=out_shape,
        in_specs=specs,
        out_specs=out_spec,
        scratch_shapes=scratch,
        input_output_aliases=aliases,
        compiler_params=params(),
        cost_estimate=BRIEF,
        name=name,
    )(*args)


def space(low, mid, high, band, base, start, size, width, **where):
    half = width // 2

    def body(refs, columns, probe, sites):
        low, mid, high, band = refs[:4]
        total = dot_t(mid[base + probe], band[sites, half : half + width])
        total += dot_t(low[probe], band[sites, :half])
        total += dot_t(high[probe], band[sites, half + width :])
        return total

    return by_columns("space", body, [low, mid, high, band], mid.shape[1], start, size, 256, width, **where)


def mix(table, blocks, width, start=0, begun=None, step=512, **where):
    rows = table.shape[0]
    flat = [piece for block in blocks.values() for piece in block]

    def body(refs, columns, probe, sites):
        taken = 1
        total = None
        for m, block in blocks.items():
            parts = [ref[:, columns] for ref in refs[taken : taken + len(block)]]
            taken += len(block)
            term = dot(refs[0][:, m * rows : (m + 1) * rows], jnp.concatenate(parts, axis=0))
            total = term if total is None else total + term
        return total if begun is None else total + refs[taken][:, columns]

    args = [table] + flat + ([] if begun is None else [begun])
    return by_columns("mix", body, args, rows, start, flat[0].shape[1], step, width, **where)


def after(value, *others):
    return lax.optimization_barrier((value,) + others)[0]


def on_device(field, time_row, sp_weight, offsets, noise):
    probes, rows, width = field.shape
    half = width // 2
    count = lax.axis_size("slot")
    sites = lax.axis_size("site")
    core = (lax.axis_index("slot") % 2).astype(jnp.int32).reshape(1)
    noise = noise[None, :]

    swap = [(i, i ^ 1) for i in range(count)]
    shifts = range(2, count, 2)
    up = [(i, i + 1) for i in range(sites - 1)]
    down = [(i + 1, i) for i in range(sites - 1)]

    def to_core(block, pieces=1):
        return [lax.ppermute(part, "slot", swap) for part in jnp.split(block, pieces, axis=0)]

    def to_chips(block):
        return [lax.ppermute(block, "slot", [(i, (i + s) % count) for i in range(count)]) for s in shifts]

    def halo(block):
        return (
            lax.ppermute(block[:, :, width - half :], "site", up),
            lax.ppermute(block[:, :, :half], "site", down),
        )

    order = ([0, 1], [0, count - 1])
    for s in shifts:
        order[0].extend([(-s) % count, (1 - s) % count])
        order[1].extend([(-s) % count, (-1 - s) % count])

    def arrived(far, pieces, *others):
        straight, crossed = {}, {}
        for k, got in enumerate(far):
            got = after(got, *others)
            straight[2 + 2 * k] = [got]
            crossed[3 + 2 * k] = to_core(got, pieces)
        return straight, crossed

    def here(own, near):
        return {0: [own], 1: near}

    firsts = probes // 2
    own, far = [], []
    rest = field
    for p in range(firsts):
        own.append(rest[p])
        far.append(to_chips(own[p]))
        rest = after(field, own[p])
        if p == 0:
            low, high = halo(rest[firsts:])

    table = time_table(time_row, core, order, rows)
    col = jnp.arange(sp_weight.shape[1], dtype=jnp.int32)
    mask = (col[None, :] >= offsets[:, None]) & (col[None, :] < offsets[:, None] + width)
    band = jnp.where(mask, sp_weight, jnp.zeros_like(sp_weight))

    near = [to_core(block) for block in own]
    columns = (probes - firsts) * width
    last = half
    cut = columns - last
    terms = (noise, field)
    image = jax.ShapeDtypeStruct(field.shape, field.dtype)

    straight, crossed = arrived(far[0], 2, table, band)
    blocks = here(own[0], near[0]) | straight | crossed
    mixed = [mix(table, blocks, width)]
    long = space(low, field, high, after(band, mixed[0]), firsts, 0, cut, width)
    far_long = to_chips(long)
    for p in range(1, firsts):
        straight, crossed = arrived(far[p], 2, mixed[-1], long)
        blocks = here(own[p], near[p]) | straight | crossed
        mixed.append(mix(table, blocks, width))

    for p in range(firsts):
        middle = mixed[p][None]
        got_low, got_high = halo(middle)
        image = space(got_low, middle, got_high, band, 0, 0, width, width, probe=p, terms=terms, image=image)
        if p == 0:
            near_long = to_core(after(long, image), 4)
            short = space(low, field, high, after(band, image), firsts, cut, last, width)
            near_short, far_short = to_core(short), to_chips(short)

    at = dict(start=cut, probe=firsts)
    begun = mix(table, here(short, after(near_short, image)), width, terms=terms, dtype=F32, **at)
    straight, crossed = arrived(far_long, 4, begun)
    straight = here(long, near_long) | straight
    sums = mix(table, straight, width, probe=firsts, terms=terms, dtype=F32)
    image = mix(table, crossed, width, probe=firsts, begun=sums, image=image)
    straight, crossed = arrived(far_short, 1, image)
    begun = mix(table, straight, width, begun=begun, dtype=F32, **at)
    return mix(table, crossed, width, begun=begun, image=image, step=256, **at)


def solution(mesh):
    in_specs = (P("grp", "slot", "site"), P(), P("site", None), P("site"), P("site"))
    out_specs = P("grp", "slot", "site")
    return jax.shard_map(
        on_device, mesh=mesh, in_specs=in_specs, out_specs=out_specs, check_vma=False
    )
```
